32 devices in a mesh: groups: 2 (over x), ctx: 8 (over z, y), chan: 2 (over core).
Axes of the slice: x: 2, y: 2, z: 4, core: 2. Of those that a mesh axis runs over, the one named last changes fastest.
Arguments:
- tokens: int32 [4, 512], P('groups', 'ctx'), parts along dimension 0, may hold values from 0 to 511
- embed_table: bfloat16 [512, 4096], replicated, may hold values from -8 to 8
- norm_gain: float32 [4096], replicated, may hold values from 0.1 to 1.9
- input_proj: bfloat16 [4096, 3, 2048], P('ctx', None, 'chan'), may hold values from -0.09375 to 0.09375
- short_filter: float32 [3, 128, 3], P(None, 'chan'), may hold values from -3.5 to 3.5
- pole_rate: float32 [128, 16], P('chan'), may hold values from 0.0005859375 to 0.2
- residue: float32 [128, 16], P('chan'), may hold values from -1.5 to 1.5
- skip_gain: float32 [2048], P('chan'), may hold values from -3 to 3
- output_proj: bfloat16 [2048, 4096], P('chan', 'ctx'), may hold values from -0.125 to 0.125
Outputs:
- block_out: bfloat16 [4, 512, 4096], P('groups', 'ctx', 'chan'), parts along dimension 0
The draws below stay inside these ranges and needn't reach their ends.
There are 2 independent parts, one for each index of `groups`. The reference program is written for one: setup_inputs(seed, part) draws one part's arguments, and reference() takes and returns one part's arrays. A program takes and returns all parts, laid end to end along the dimension named above; an argument that names none is the same for every part. Nothing has to cross between parts.
All inputs are finite; a program needn't handle non-finite values.
Results may differ from the reference program's by a relative error of at most 0.0078.
Values may be sent and summed in bfloat16 or wider, within the bound.
A program may use at most 128 MiB of HBM per device.

```python
import math
import jax
import jax.numpy as jnp
from jax import lax

D = 4096
VOCAB = 512
HC = 2048
GS = 16
POLES = 16
KS = 3
GEN = 2
LEN = 512


def draw_embed_table(key, part):
    first_key, second_key, third_key = jax.random.split(key, 3)
    row_scale = 10.0 ** jax.random.uniform(first_key, (VOCAB, 1), jnp.float32)
    col_scale = 10.0 ** jax.random.uniform(second_key, (1, D), jnp.float32)
    values = jnp.clip(jax.random.normal(third_key, (VOCAB, D), jnp.float32), -4.0, 4.0)
    return (0.02 * values * row_scale * col_scale).astype(jnp.bfloat16)


def draw_pole_rate(key, part):
    first_key, second_key, third_key, fourth_key = jax.random.split(key, 4)
    shape = (HC // GS, POLES)
    slow_rate = jnp.exp(jax.random.uniform(first_key, shape, jnp.float32, math.log(0.3), math.log(2.0))) / LEN
    middle_rate = jnp.exp(jax.random.uniform(fourth_key, shape, jnp.float32, math.log(2.0) - math.log(LEN), math.log(0.02)))
    fast_rate = jnp.exp(jax.random.uniform(second_key, shape, jnp.float32, math.log(0.02), math.log(0.2)))
    slow_share = 0.5
    middle_share = 0.25
    picked = jax.random.uniform(third_key, shape, jnp.float32)
    rate = jnp.where(picked < slow_share, slow_rate, jnp.where(picked < slow_share + middle_share, middle_rate, fast_rate))
    return rate.astype(jnp.float32)


def with_ends(result, key, smallest, high):
    extent = result.shape
    spot = [jax.random.randint(jax.random.fold_in(key, axis), (), 0, extent[axis]) for axis in range(len(extent))]
    result = result.at[tuple(spot)].set(smallest)
    longest = extent.index(max(extent))
    spot[longest] = (spot[longest] + 1) % extent[longest]
    return result.at[tuple(spot)].set(high)


def block_levels(own_key, extent, shards, low, top_value):
    loudness, own = 1.0, jax.random.fold_in(own_key, 6)
    for axis_at, shards_of in shards:
        draws = jnp.exp(jax.random.uniform(jax.random.fold_in(own, axis_at), (shards_of,), jnp.float32, low / len(shards), top_value / len(shards)))
        loudness = loudness * jnp.repeat(draws, extent[axis_at] // shards_of).reshape([-1 if axis == axis_at else 1 for axis in range(len(extent))])
    return loudness


def centred(stream_key, extent, scale, reach, shards=(), dtype=jnp.bfloat16):
    array = jax.random.normal(stream_key, extent, jnp.float32) * scale
    if len(shards) > 0:
        array = block_levels(stream_key, extent, shards, -0.22, 0.18) * array
    return jnp.clip(array, min=-reach, max=reach).astype(dtype)


def setup_inputs(seed: int = 0, part: int = 0) -> dict:
    key_list = jax.random.split(jax.random.key(seed), 10)
    part_splits = jax.random.split(jax.random.fold_in(key_list[9], part), 10)
    return {
        "tokens": with_ends(jax.random.randint(part_splits[0], (GEN, LEN), 0, VOCAB), jax.random.fold_in(part_splits[0], 1), 0, VOCAB - 1).astype(jnp.int32),
        "embed_table": draw_embed_table(jax.random.fold_in(key_list[9], 71), part),
        "norm_gain": jnp.clip(1.0 + 0.18 * jax.random.normal(key_list[2], (D,), jnp.float32), 0.1, 1.9),
        "input_proj": centred(key_list[3], (D, 3, HC), D ** -0.5, 0.09375, ((0, 8), (2, 2))),
        "short_filter": centred(key_list[4], (3, HC // GS, KS), 0.6, 3.5, ((1, 2),), jnp.float32),
        "pole_rate": draw_pole_rate(jax.random.fold_in(key_list[9], 71), part),
        "residue": centred(key_list[6], (HC // GS, POLES), 0.25, 1.5, ((0, 2),), jnp.float32),
        "skip_gain": centred(key_list[7], (HC,), 0.5, 3.0, ((0, 2),), jnp.float32),
        "output_proj": centred(key_list[8], (HC, D), HC ** -0.5, 0.125, ((0, 2), (1, 8))),
    }


epsilon = 1e-06

def reference(tokens, embed_table, norm_gain, input_proj, short_filter, pole_rate, residue, skip_gain, output_proj):
    embedded = jnp.take(embed_table, tokens, axis=0)
    widened = embedded.astype(jnp.float32)
    inv_rms = lax.rsqrt(lax.optimization_barrier(jnp.mean(widened * widened, axis=-1, keepdims=True)) + epsilon)
    normed = (widened * inv_rms * norm_gain).astype(jnp.bfloat16)
    flat_rows = normed.reshape(GEN * LEN, D)
    summed = jnp.dot(flat_rows, input_proj.reshape(D, 3 * HC), preferred_element_type=jnp.float32)
    projected = summed.astype(jnp.bfloat16).reshape(GEN, LEN, 3, HC)
    widened_proj = projected.astype(jnp.float32)
    taps_full = jnp.repeat(short_filter, GS, axis=1)
    filtered = jnp.zeros((GEN, LEN, 3, HC), jnp.float32)
    for lag in range(KS):
        shifted = jnp.pad(widened_proj, ((0, 0), (lag, 0), (0, 0), (0, 0)))[:, :LEN]
        filtered = filtered + taps_full[:, :, lag] * shifted
    query_part = filtered[:, :, 0]
    product = filtered[:, :, 1] * filtered[:, :, 2]
    pole_decay = jnp.exp(-pole_rate)
    pole_amp = residue * jnp.sqrt(-jnp.expm1(-2.0 * pole_rate))
    decay_full = jnp.repeat(pole_decay, GS, axis=0)
    amp_full = jnp.repeat(pole_amp, GS, axis=0)

    def advance(carried, column):
        carried = decay_full * carried + column[:, :, None]
        return (carried, lax.optimization_barrier(jnp.sum(carried * amp_full, axis=-1)))
    start_state = jnp.zeros((GEN, HC, POLES), jnp.float32)
    final_state, history = lax.scan(advance, start_state, jnp.moveaxis(product, 1, 0))
    long_conv = jnp.moveaxis(history, 0, 1)
    gated = (query_part * (long_conv + skip_gain * product)).astype(jnp.bfloat16)
    mixed = jnp.dot(gated.reshape(GEN * LEN, HC), output_proj, preferred_element_type=jnp.float32)
    block_out = (widened.reshape(GEN * LEN, D) + mixed).astype(jnp.bfloat16)
    return block_out.reshape(GEN, LEN, D)
```

```python
import functools

import jax
import jax.numpy as jnp
from jax import lax
from jax.experimental import pallas as pl
from jax.experimental.pallas import tpu as pltpu
from jax.sharding import PartitionSpec as P

EPSILON = 1e-06
LANES = 128
MESH = pl.DeviceIdType.MESH
F32 = jnp.float32
BF16 = jnp.bfloat16


def remote(src, dst, send_sem, recv_sem, where):
    return pltpu.make_async_remote_copy(
        src_ref=src,
        dst_ref=dst,
        send_sem=send_sem,
        recv_sem=recv_sem,
        device_id=where,
        device_id_type=MESH,
    )


def kernel(
    sizes,
    tok_ref,
    norm_ref,
    w_ref,
    taps_ref,
    rate_ref,
    amp_ref,
    skip_ref,
    wout_ref,
    table_ref,
    out_ref,
    tok_all,
    tok_col,
    part_y,
    part_own,
    recv_y,
    recv_r,
    recv_l,
    sum_z,
    vocab_proj,
    toeplitz,
    conv,
    gathered,
    acc,
    recv_c,
    obuf,
    land,
    table_cols,
    tok_send,
    tok_recv,
    ysend,
    yrecv,
    zsend,
    rrecv,
    lrecv,
    gsend,
    grecv,
    ar_send,
    al_send,
    ay_send,
    arecv,
    csend,
    crecv,
    osend,
    orecv,
    local_sem,
):
    groups, ctx, chans, ny, group_size = sizes
    nz = ctx // ny
    genomes, local_len = tok_ref.shape
    length = local_len * ctx
    rows = norm_ref.shape[0]
    vocab = rows * groups
    cols = wout_ref.shape[1]
    poles = rate_ref.shape[1]
    filters = rate_ref.shape[0]
    half = length // chans
    per = ctx // chans

    gi = lax.axis_index("groups")
    me = lax.axis_index("ctx")
    ci = lax.axis_index("chan")
    y = lax.rem(me, ny)
    z = me // ny
    other_y = z * ny + (ny - 1 - y)
    right, left = me + ny, me - ny
    dest_chan = me // per

    barrier = pltpu.get_barrier_semaphore()

    def greet(where):
        pl.semaphore_signal(barrier, inc=1, device_id=where, device_id_type=MESH)

    for off in range(1, ctx):
        greet({"ctx": lax.rem(me + off, ctx)})
    for off in range(1, groups):
        greet({"groups": lax.rem(gi + off, groups)})
    greet({"chan": 1 - ci})
    for q in range(per):
        target = ci * per + q

        @pl.when(jnp.logical_or(target != me, dest_chan != ci))
        def _():
            greet({"ctx": target, "chan": dest_chan})

    table_copy = pltpu.make_async_copy(
        table_ref.at[:, pl.ds(pl.multiple_of(me * cols, LANES), cols)], table_cols, local_sem.at[0]
    )
    table_copy.start()
    self_target = jnp.where(dest_chan == ci, 1, 0)
    pl.semaphore_wait(barrier, ctx - 1 + groups - 1 + 1 + per - self_target)

    tok_all[me] = tok_ref[...]
    for off in range(1, ctx):
        peer = lax.rem(me + off, ctx)
        remote(
            tok_ref, tok_all.at[me], tok_send.at[off], tok_recv.at[me], {"ctx": peer}
        ).start()

    def project(block, branch):
        columns = pl.ds(pl.multiple_of(block * LANES, LANES), LANES)
        return jnp.dot(norm_ref[...], w_ref[branch, :, columns], preferred_element_type=F32)

    order = []
    for step in range((nz + 1) // 2):
        order.append(nz - 1 - step)
        if step != nz - 1 - step:
            order.append(step)
    if ny == 2:
        for dz in order:
            for branch in range(3):
                part_y[dz, :, branch * LANES : (branch + 1) * LANES] = project(
                    dz * ny + 1 - y, branch
                ).astype(BF16)
            remote(
                part_y.at[dz], recv_y.at[dz], ysend.at[dz], yrecv.at[dz], {"ctx": other_y}
            ).start()
    for dz in order:
        for branch in range(3):
            part_own[dz, :, branch * LANES : (branch + 1) * LANES] = project(dz * ny + y, branch)

    def with_y(dz):
        value = part_own[dz]
        if ny == 2:
            remote(
                part_y.at[dz], recv_y.at[dz], ysend.at[dz], yrecv.at[dz], {"ctx": other_y}
            ).wait_recv()
            value = value + recv_y[dz].astype(F32)
        return value

    def right_copy(dz):
        return remote(sum_z.at[dz], recv_r.at[dz], zsend.at[dz], rrecv.at[dz], {"ctx": right})

    def left_copy(dz):
        return remote(sum_z.at[dz], recv_l.at[dz], zsend.at[dz], lrecv.at[dz], {"ctx": left})

    for step in range(nz - 1):
        dr, dl = nz - 1 - step, step

        @pl.when(z < dr)
        def _():
            part_own[dr] = with_y(dr)

            @pl.when(z > 0)
            def _():
                right_copy(dr).wait_recv()
                part_own[dr] = part_own[dr] + recv_r[dr].astype(F32)

            sum_z[dr] = part_own[dr].astype(BF16)
            right_copy(dr).start()

        @pl.when(z > dl)
        def _():
            part_own[dl] = with_y(dl)

            @pl.when(z < nz - 1)
            def _():
                left_copy(dl).wait_recv()
                part_own[dl] = part_own[dl] + recv_l[dl].astype(F32)

            sum_z[dl] = part_own[dl].astype(BF16)
            left_copy(dl).start()

    width = length + LANES
    lag = length - 1 - lax.broadcasted_iota(jnp.int32, (poles, width), 1)
    lag_f = jnp.maximum(lag, 0).astype(F32)
    for f in range(filters):
        taps = jnp.sum(amp_ref[f] * jnp.exp(-rate_ref[f] * lag_f), axis=0, keepdims=True)
        taps = jnp.where(lag[:1] >= 0, taps, 0.0)
        rolled = pltpu.roll(
            jnp.broadcast_to(taps, (LANES, width)), width - (LANES - 1), 1, stride=1, stride_axis=0
        )
        toeplitz[f] = rolled[:, :length].astype(BF16)

    for off in range(1, ctx):
        peer = lax.rem(me + off, ctx)
        remote(
            tok_ref, tok_all.at[peer], tok_send.at[off], tok_recv.at[peer], {"ctx": peer}
        ).wait_recv()
    for b in range(genomes):
        line = jnp.concatenate([tok_all[i, b : b + 1, :] for i in range(ctx)], axis=1)
        tok_col[b] = jnp.transpose(jnp.broadcast_to(line, (LANES, length)))

    own = with_y(z)
    part_own[z] = own

    @pl.when(z > 0)
    def _():
        right_copy(z).wait_recv()
        part_own[z] = part_own[z] + recv_r[z].astype(F32)

    @pl.when(z < nz - 1)
    def _():
        left_copy(z).wait_recv()
        part_own[z] = part_own[z] + recv_l[z].astype(F32)

    vocab_proj[gi] = part_own[z].astype(BF16)

    def group_copy(off):
        return remote(
            vocab_proj.at[gi],
            vocab_proj.at[gi],
            gsend.at[off],
            grecv.at[gi],
            {"groups": lax.rem(gi + off, groups)},
        )

    for off in range(1, groups):
        group_copy(off).start()
    for off in range(1, groups):
        peer = lax.rem(gi + off, groups)
        remote(
            vocab_proj.at[peer],
            vocab_proj.at[peer],
            gsend.at[off],
            grecv.at[peer],
            {"groups": peer},
        ).wait_recv()

    table_proj = vocab_proj[...].reshape(vocab, 3 * LANES)

    def onehot(columns):
        parts = []
        for v in range(vocab // LANES):
            ids = lax.broadcasted_iota(jnp.int32, columns.shape, 1) + v * LANES
            parts.append(jnp.where(columns == ids, 1.0, 0.0).astype(BF16))
        return jnp.concatenate(parts, axis=1)

    row_ids = lax.broadcasted_iota(jnp.int32, (length, LANES), 0)
    queries, products = [], []
    for b in range(genomes):
        projected = jnp.dot(onehot(tok_col[b]), table_proj, preferred_element_type=F32)
        filtered = []
        for branch in range(3):
            value = projected[:, branch * LANES : (branch + 1) * LANES]
            total = taps_ref[branch * 3 : branch * 3 + 1, :] * value
            for k in (1, 2):
                shifted = jnp.where(row_ids >= k, pltpu.roll(value, k, 0), 0.0)
                at = branch * 3 + k
                total = total + taps_ref[at : at + 1, :] * shifted
            filtered.append(total)
        queries.append(filtered[0])
        products.append(filtered[1] * filtered[2])
    both = jnp.concatenate(products, axis=1)
    lane_filter = lax.rem(
        lax.broadcasted_iota(jnp.int32, (length, genomes * LANES), 1), LANES
    ) // group_size
    blocks = length // LANES
    for f in range(filters):
        masked = jnp.where(lane_filter == f, both, 0.0).astype(BF16)
        for i in range(blocks):
            term = jnp.dot(
                toeplitz[f, :, (blocks - 1 - i) * LANES :],
                masked[: (i + 1) * LANES],
                preferred_element_type=F32,
            )
            at = slice(i * LANES, (i + 1) * LANES)
            conv[at, :] = term if f == 0 else conv[at, :] + term
    for b in range(genomes):
        long_conv = conv[:, b * LANES : (b + 1) * LANES]
        gated = queries[b] * (long_conv + skip_ref[...] * products[b])
        gathered[me, b] = gated.astype(BF16)

    def along(slot, sems, where):
        return remote(
            gathered.at[slot], gathered.at[slot], sems.at[slot], arecv.at[slot], {"ctx": where}
        )

    @pl.when(z < nz - 1)
    def _():
        along(me, ar_send, right).start()

    @pl.when(z > 0)
    def _():
        along(me, al_send, left).start()

    if ny == 2:
        along(me, ay_send, other_y).start()

    acc[...] = jnp.zeros_like(acc)

    def multiply(slot):
        weight = wout_ref[pl.ds(pl.multiple_of(slot * LANES, LANES), LANES), :]
        for b in range(genomes):
            acc[b] = acc[b] + jnp.dot(gathered[slot, b], weight, preferred_element_type=F32)

    multiply(me)

    @pl.loop(1, nz)
    def _(step):
        from_left = me - step * ny
        from_right = me + step * ny

        @pl.when(from_left >= 0)
        def _():
            along(from_left, ar_send, right).wait_recv()

            @pl.when(z < nz - 1)
            def _():
                along(from_left, ar_send, right).start()

            if ny == 2:
                along(from_left, ay_send, other_y).start()

        @pl.when(from_right < ctx)
        def _():
            along(from_right, al_send, left).wait_recv()

            @pl.when(z > 0)
            def _():
                along(from_right, al_send, left).start()

            if ny == 2:
                along(from_right, ay_send, other_y).start()

        @pl.when(from_left >= 0)
        def _():
            multiply(from_left)

        @pl.when(from_right < ctx)
        def _():
            multiply(from_right)

    if ny == 2:

        @pl.loop(0, nz)
        def _(step):
            twin_z = lax.rem(z + step, nz)
            slot = twin_z * ny + (1 - y)
            along(slot, ay_send, other_y).wait_recv()
            multiply(slot)

    swap = remote(
        acc.at[:, pl.ds(pl.multiple_of((1 - ci) * half, LANES), half), :],
        recv_c,
        csend.at[0],
        crecv.at[0],
        {"chan": 1 - ci},
    )
    swap.start()
    table_copy.wait()
    mine = pl.ds(pl.multiple_of(ci * half, LANES), half)
    for b in range(genomes):
        land_tok = tok_col[b, mine, :]
        acc[b, mine, :] = acc[b, mine, :] + jnp.dot(
            onehot(land_tok), table_cols[...], preferred_element_type=F32
        )
    swap.wait()
    for b in range(genomes):
        obuf[b] = (acc[b, mine, :] + recv_c[b]).astype(BF16)

    def out_copy(q, source_slot):
        return remote(
            obuf.at[:, pl.ds(q * local_len, local_len), :],
            land.at[source_slot],
            osend.at[q],
            orecv.at[source_slot],
            {"ctx": ci * per + q, "chan": dest_chan},
        )

    def is_self(q):
        return jnp.logical_and(ci * per + q == me, dest_chan == ci)

    my_slot = lax.rem(me, per)
    for q in range(per):

        @pl.when(jnp.logical_not(is_self(q)))
        def _():
            out_copy(q, my_slot).start()

        @pl.when(is_self(q))
        def _():
            land[my_slot] = obuf[:, q * local_len : (q + 1) * local_len, :]

    for q in range(per):

        @pl.when(jnp.logical_not(is_self(q)))
        def _():
            out_copy(q, q).wait_recv()

        out_ref[:, :, q * cols : (q + 1) * cols] = land[q]

    for q in range(per):

        @pl.when(jnp.logical_not(is_self(q)))
        def _():
            out_copy(q, my_slot).wait_send()

    for off in range(1, ctx):
        remote(
            tok_ref, tok_all.at[me], tok_send.at[off], tok_recv.at[me], {"ctx": lax.rem(me + off, ctx)}
        ).wait_send()
    for off in range(1, groups):
        group_copy(off).wait_send()
    for dz in range(nz):
        if ny == 2:
            remote(
                part_y.at[dz], recv_y.at[dz], ysend.at[dz], yrecv.at[dz], {"ctx": other_y}
            ).wait_send()

        @pl.when(z < dz)
        def _():
            right_copy(dz).wait_send()

        @pl.when(z > dz)
        def _():
            left_copy(dz).wait_send()

        slot = dz * ny + y

        @pl.when(jnp.logical_and(dz <= z, z < nz - 1))
        def _():
            along(slot, ar_send, right).wait_send()

        @pl.when(jnp.logical_and(dz >= z, z > 0))
        def _():
            along(slot, al_send, left).wait_send()

        if ny == 2:
            along(slot, ay_send, other_y).wait_send()


def body(
    groups,
    ctx,
    chans,
    tokens,
    embed_table,
    norm_gain,
    input_proj,
    short_filter,
    pole_rate,
    residue,
    skip_gain,
    output_proj,
):
    genomes, local_len = tokens.shape
    length = local_len * ctx
    features, branches, channels = input_proj.shape
    vocab = embed_table.shape[0]
    filter_count, poles = pole_rate.shape
    group_size = channels // filter_count
    share = channels // ctx
    filters = filter_count // ctx
    cols = output_proj.shape[1]
    rows = vocab // groups
    ny = 2 if ctx % 2 == 0 and ctx <= 8 else 1
    nz = ctx // ny
    taps = short_filter.shape[2]
    me = lax.axis_index("ctx")
    gi = lax.axis_index("groups")
    half = length // chans
    per = ctx // chans

    own_rows = lax.dynamic_slice_in_dim(embed_table, gi * rows, rows, 0)
    wide = own_rows.astype(F32)
    inv_rms = lax.rsqrt(jnp.mean(wide * wide, axis=-1, keepdims=True) + EPSILON)
    own_feats = lax.dynamic_slice_in_dim(own_rows, me * features, features, 1).astype(F32)
    gain = lax.dynamic_slice_in_dim(norm_gain, me * features, features, 0)
    normed = (own_feats * inv_rms * gain).astype(BF16)

    def padded(array):
        if share == LANES:
            return array
        cut = array.reshape(array.shape[:-1] + (ctx, share))
        pads = [(0, 0)] * (cut.ndim - 1) + [(0, LANES - share)]
        return jnp.pad(cut, pads).reshape(array.shape[:-1] + (ctx * LANES,))

    def own_share(array):
        wide_array = jnp.repeat(array, group_size, axis=-1)
        return jnp.pad(wide_array, [(0, 0)] * (array.ndim - 1) + [(0, LANES - share)])

    weights = padded(jnp.transpose(input_proj, (1, 0, 2)))
    out_weights = output_proj
    if share != LANES:
        out_weights = jnp.pad(
            output_proj.reshape(ctx, share, cols), ((0, 0), (0, LANES - share), (0, 0))
        ).reshape(ctx * LANES, cols)
    own_filter = lax.dynamic_slice_in_dim(short_filter, me * filters, filters, 1)
    tap_rows = own_share(jnp.transpose(own_filter, (0, 2, 1)).reshape(branches * taps, filters))
    rate = lax.dynamic_slice_in_dim(pole_rate, me * filters, filters, 0)
    own_residue = lax.dynamic_slice_in_dim(residue, me * filters, filters, 0)
    amp = own_residue * jnp.sqrt(-jnp.expm1(-2.0 * rate))
    skip = lax.dynamic_slice_in_dim(skip_gain, me * share, share, 0)
    skip = jnp.pad(skip, (0, LANES - share)).reshape(1, LANES)

    vmem = pl.BlockSpec(memory_space=pltpu.VMEM)
    dma = pltpu.SemaphoreType.DMA
    wide_lanes = 3 * LANES
    result = pl.pallas_call(
        functools.partial(kernel, (groups, ctx, chans, ny, group_size)),
        out_shape=jax.ShapeDtypeStruct((genomes, local_len, cols * per), BF16),
        in_specs=[vmem] * 8 + [pl.BlockSpec(memory_space=pl.ANY)],
        out_specs=vmem,
        scratch_shapes=[
            pltpu.VMEM((ctx, genomes, local_len), jnp.int32),
            pltpu.VMEM((genomes, length, LANES), jnp.int32),
            pltpu.VMEM((nz, rows, wide_lanes), BF16),
            pltpu.VMEM((nz, rows, wide_lanes), F32),
            pltpu.VMEM((nz, rows, wide_lanes), BF16),
            pltpu.VMEM((nz, rows, wide_lanes), BF16),
            pltpu.VMEM((nz, rows, wide_lanes), BF16),
            pltpu.VMEM((nz, rows, wide_lanes), BF16),
            pltpu.VMEM((groups, rows, wide_lanes), BF16),
            pltpu.VMEM((filters, LANES, length), BF16),
            pltpu.VMEM((length, genomes * LANES), F32),
            pltpu.VMEM((ctx, genomes, length, LANES), BF16),
            pltpu.VMEM((genomes, length, cols), F32),
            pltpu.VMEM((genomes, half, cols), F32),
            pltpu.VMEM((genomes, half, cols), BF16),
            pltpu.VMEM((per, genomes, local_len, cols), BF16),
            pltpu.VMEM((vocab, cols), BF16),
            dma((ctx,)),
            dma((ctx,)),
            dma((nz,)),
            dma((nz,)),
            dma((nz,)),
            dma((nz,)),
            dma((nz,)),
            dma((groups,)),
            dma((groups,)),
            dma((ctx,)),
            dma((ctx,)),
            dma((ctx,)),
            dma((ctx,)),
            dma((1,)),
            dma((1,)),
            dma((per,)),
            dma((per,)),
            dma((1,)),
        ],
        compiler_params=pltpu.CompilerParams(
            collective_id=0, has_side_effects=True, vmem_limit_bytes=50 * 1024 * 1024
        ),
    )(
        tokens,
        normed,
        weights,
        tap_rows,
        rate[:, :, None],
        amp[:, :, None],
        skip,
        out_weights,
        embed_table,
    )
    return result


def solution(mesh):
    sizes = mesh.shape
    return jax.shard_map(
        functools.partial(body, sizes["groups"], sizes["ctx"], sizes["chan"]),
        mesh=mesh,
        in_specs=(
            P("groups", "ctx"),
            P(),
            P(),
            P("ctx", None, "chan"),
            P(None, "chan", None),
            P("chan", None),
            P("chan", None),
            P("chan"),
            P("chan", "ctx"),
        ),
        out_specs=P("groups", "ctx", "chan"),
        check_vma=False,
    )
```

```python
import functools

import jax
import jax.numpy as jnp
from jax import lax
from jax.experimental import pallas as pl
from jax.experimental.pallas import tpu as pltpu
from jax.sharding import PartitionSpec as P

EPSILON = 1e-06
LANES = 128
PIECES = 2
MESH = pl.DeviceIdType.MESH
F32 = jnp.float32
BF16 = jnp.bfloat16


def remote(src, dst, send_sem, recv_sem, where):
    return pltpu.make_async_remote_copy(
        src_ref=src,
        dst_ref=dst,
        send_sem=send_sem,
        recv_sem=recv_sem,
        device_id=where,
        device_id_type=MESH,
    )


def kernel(
    sizes,
    tok_ref,
    norm_ref,
    w_ref,
    taps_ref,
    rate_ref,
    amp_ref,
    skip_ref,
    wout_ref,
    table_ref,
    out_ref,
    tok_all,
    tok_col,
    part_y,
    part_own,
    recv_y,
    recv_r,
    recv_l,
    sum_z,
    vocab_proj,
    toeplitz,
    conv,
    gathered,
    acc,
    recv_c,
    obuf,
    land,
    table_cols,
    tok_send,
    tok_recv,
    ysend,
    yrecv,
    zsend,
    rrecv,
    lrecv,
    gsend,
    grecv,
    ar_send,
    al_send,
    ay_send,
    arecv,
    csend,
    crecv,
    osend,
    orecv,
    local_sem,
):
    groups, ctx, chans, ny, group_size = sizes
    nz = ctx // ny
    genomes, local_len = tok_ref.shape
    length = local_len * ctx
    rows = norm_ref.shape[0]
    vocab = rows * groups
    cols = wout_ref.shape[1]
    poles = rate_ref.shape[1]
    filters = rate_ref.shape[0]
    half = length // chans
    per = ctx // chans

    gi = lax.axis_index("groups")
    me = lax.axis_index("ctx")
    ci = lax.axis_index("chan")
    y = lax.rem(me, ny)
    z = me // ny
    other_y = z * ny + (ny - 1 - y)
    right, left = me + ny, me - ny
    dest_chan = me // per

    barrier = pltpu.get_barrier_semaphore()

    def greet(where):
        pl.semaphore_signal(barrier, inc=1, device_id=where, device_id_type=MESH)

    for off in range(1, ctx):
        greet({"ctx": lax.rem(me + off, ctx)})
    for off in range(1, groups):
        greet({"groups": lax.rem(gi + off, groups)})
    greet({"chan": 1 - ci})
    for q in range(per):
        target = ci * per + q

        @pl.when(jnp.logical_or(target != me, dest_chan != ci))
        def _():
            greet({"ctx": target, "chan": dest_chan})

    table_copy = pltpu.make_async_copy(
        table_ref.at[:, pl.ds(pl.multiple_of(me * cols, LANES), cols)], table_cols, local_sem.at[0]
    )
    table_copy.start()
    self_target = jnp.where(dest_chan == ci, 1, 0)
    pl.semaphore_wait(barrier, ctx - 1 + groups - 1 + 1 + per - self_target)

    tok_all[me] = tok_ref[...]
    for off in range(1, ctx):
        peer = lax.rem(me + off, ctx)
        remote(
            tok_ref, tok_all.at[me], tok_send.at[off], tok_recv.at[me], {"ctx": peer}
        ).start()

    pieces = part_own.shape[1]
    piece = rows // pieces

    def project(h, block, branch):
        columns = pl.ds(pl.multiple_of(block * LANES, LANES), LANES)
        return jnp.dot(
            norm_ref[h * piece : (h + 1) * piece, :],
            w_ref[branch, :, columns],
            preferred_element_type=F32,
        )

    order = []
    for step in range((nz + 1) // 2):
        order.append(nz - 1 - step)
        if step != nz - 1 - step:
            order.append(step)

    def y_copy(dz, h):
        return remote(
            part_y.at[dz, h], recv_y.at[dz, h], ysend.at[dz, h], yrecv.at[dz, h], {"ctx": other_y}
        )

    for h in range(pieces):
        if ny == 2:
            for dz in order:
                for branch in range(3):
                    part_y[dz, h, :, branch * LANES : (branch + 1) * LANES] = project(
                        h, dz * ny + 1 - y, branch
                    ).astype(BF16)
                y_copy(dz, h).start()
    for h in range(pieces):
        for dz in order:
            for branch in range(3):
                part_own[dz, h, :, branch * LANES : (branch + 1) * LANES] = project(
                    h, dz * ny + y, branch
                )

    def with_y(dz, h):
        value = part_own[dz, h]
        if ny == 2:
            y_copy(dz, h).wait_recv()
            value = value + recv_y[dz, h].astype(F32)
        return value

    def right_copy(dz, h):
        return remote(
            sum_z.at[dz, h], recv_r.at[dz, h], zsend.at[dz, h], rrecv.at[dz, h], {"ctx": right}
        )

    def left_copy(dz, h):
        return remote(
            sum_z.at[dz, h], recv_l.at[dz, h], zsend.at[dz, h], lrecv.at[dz, h], {"ctx": left}
        )

    def sum_step(h, step):
        dr, dl = nz - 1 - step, step

        @pl.when(z < dr)
        def _():
            part_own[dr, h] = with_y(dr, h)

            @pl.when(z > 0)
            def _():
                right_copy(dr, h).wait_recv()
                part_own[dr, h] = part_own[dr, h] + recv_r[dr, h].astype(F32)

            sum_z[dr, h] = part_own[dr, h].astype(BF16)
            right_copy(dr, h).start()

        @pl.when(z > dl)
        def _():
            part_own[dl, h] = with_y(dl, h)

            @pl.when(z < nz - 1)
            def _():
                left_copy(dl, h).wait_recv()
                part_own[dl, h] = part_own[dl, h] + recv_l[dl, h].astype(F32)

            sum_z[dl, h] = part_own[dl, h].astype(BF16)
            left_copy(dl, h).start()

    def group_copy(off, h, source, peer):
        return remote(
            vocab_proj.at[source, h],
            vocab_proj.at[source, h],
            gsend.at[off, h],
            grecv.at[source, h],
            {"groups": peer},
        )

    def finish(h):
        part_own[z, h] = with_y(z, h)

        @pl.when(z > 0)
        def _():
            right_copy(z, h).wait_recv()
            part_own[z, h] = part_own[z, h] + recv_r[z, h].astype(F32)

        @pl.when(z < nz - 1)
        def _():
            left_copy(z, h).wait_recv()
            part_own[z, h] = part_own[z, h] + recv_l[z, h].astype(F32)

        vocab_proj[gi, h] = part_own[z, h].astype(BF16)
        for off in range(1, groups):
            group_copy(off, h, gi, lax.rem(gi + off, groups)).start()

    width = length + LANES
    lag = length - 1 - lax.broadcasted_iota(jnp.int32, (poles, width), 1)
    lag_f = jnp.maximum(lag, 0).astype(F32)

    def long_filter(f):
        taps = jnp.sum(amp_ref[f] * jnp.exp(-rate_ref[f] * lag_f), axis=0, keepdims=True)
        taps = jnp.where(lag[:1] >= 0, taps, 0.0)
        rolled = pltpu.roll(
            jnp.broadcast_to(taps, (LANES, width)), width - (LANES - 1), 1, stride=1, stride_axis=0
        )
        toeplitz[f] = rolled[:, :length].astype(BF16)

    steps = []
    for h in range(pieces):
        for step in range(nz - 1):
            steps.append((sum_step, (h, step)))
            if step == 0 and h > 0:
                steps.append((finish, (h - 1,)))
    waiting = list(range(filters))
    for action, arguments in steps:
        action(*arguments)
        for f in waiting[:2]:
            long_filter(f)
        waiting = waiting[2:]
    for f in waiting:
        long_filter(f)

    for off in range(1, ctx):
        peer = lax.rem(me + off, ctx)
        remote(
            tok_ref, tok_all.at[peer], tok_send.at[off], tok_recv.at[peer], {"ctx": peer}
        ).wait_recv()
    for b in range(genomes):
        line = jnp.concatenate([tok_all[i, b : b + 1, :] for i in range(ctx)], axis=1)
        tok_col[b] = jnp.transpose(jnp.broadcast_to(line, (LANES, length)))

    finish(pieces - 1)
    for h in range(pieces):
        for off in range(1, groups):
            peer = lax.rem(gi + off, groups)
            group_copy(off, h, peer, peer).wait_recv()

    table_proj = vocab_proj[...].reshape(vocab, 3 * LANES)

    def onehot(columns):
        parts = []
        for v in range(vocab // LANES):
            ids = lax.broadcasted_iota(jnp.int32, columns.shape, 1) + v * LANES
            parts.append(jnp.where(columns == ids, 1.0, 0.0).astype(BF16))
        return jnp.concatenate(parts, axis=1)

    row_ids = lax.broadcasted_iota(jnp.int32, (length, LANES), 0)
    lane_filter = lax.broadcasted_iota(jnp.int32, (length, LANES), 1) // group_size
    blocks = length // LANES

    def along(slot, b, sems, where):
        return remote(
            gathered.at[slot, b],
            gathered.at[slot, b],
            sems.at[slot, b],
            arecv.at[slot, b],
            {"ctx": where},
        )

    for b in range(genomes):
        projected = jnp.dot(onehot(tok_col[b]), table_proj, preferred_element_type=F32)
        filtered = []
        for branch in range(3):
            value = projected[:, branch * LANES : (branch + 1) * LANES]
            total = taps_ref[branch * 3 : branch * 3 + 1, :] * value
            for k in (1, 2):
                shifted = jnp.where(row_ids >= k, pltpu.roll(value, k, 0), 0.0)
                at = branch * 3 + k
                total = total + taps_ref[at : at + 1, :] * shifted
            filtered.append(total)
        product = filtered[1] * filtered[2]
        for f in range(filters):
            masked = jnp.where(lane_filter == f, product, 0.0).astype(BF16)
            for i in range(blocks):
                term = jnp.dot(
                    toeplitz[f, :, (blocks - 1 - i) * LANES :],
                    masked[: (i + 1) * LANES],
                    preferred_element_type=F32,
                )
                at = slice(i * LANES, (i + 1) * LANES)
                conv[at, :] = term if f == 0 else conv[at, :] + term
        gated = filtered[0] * (conv[...] + skip_ref[...] * product)
        gathered[me, b] = gated.astype(BF16)

        @pl.when(z < nz - 1)
        def _():
            along(me, b, ar_send, right).start()

        @pl.when(z > 0)
        def _():
            along(me, b, al_send, left).start()

        if ny == 2:
            along(me, b, ay_send, other_y).start()

    def block_product(slot, b):
        weight = wout_ref[pl.ds(pl.multiple_of(slot * LANES, LANES), LANES), :]
        return jnp.dot(gathered[slot, b], weight, preferred_element_type=F32)

    mine = pl.ds(pl.multiple_of(ci * half, LANES), half)
    table_copy.wait()
    for b in range(genomes):
        acc[b] = block_product(me, b)
        acc[b, mine, :] = acc[b, mine, :] + jnp.dot(
            onehot(tok_col[b, mine, :]), table_cols[...], preferred_element_type=F32
        )

    def multiply(slot, b):
        acc[b] = acc[b] + block_product(slot, b)

    def z_step(b, step):
        from_left = me - step * ny
        from_right = me + step * ny

        @pl.when(from_left >= 0)
        def _():
            along(from_left, b, ar_send, right).wait_recv()

            @pl.when(z < nz - 1)
            def _():
                along(from_left, b, ar_send, right).start()

            if ny == 2:
                along(from_left, b, ay_send, other_y).start()

        @pl.when(from_right < ctx)
        def _():
            along(from_right, b, al_send, left).wait_recv()

            @pl.when(z > 0)
            def _():
                along(from_right, b, al_send, left).start()

            if ny == 2:
                along(from_right, b, ay_send, other_y).start()

        @pl.when(from_left >= 0)
        def _():
            multiply(from_left, b)

        @pl.when(from_right < ctx)
        def _():
            multiply(from_right, b)

    def y_step(b):
        if ny == 1:
            return
        for step in range(nz):
            for toward in (-1, 1) if step > 0 else (1,):
                twin_z = z + toward * step

                @pl.when(jnp.logical_and(twin_z >= 0, twin_z < nz))
                def _():
                    slot = twin_z * ny + (1 - y)
                    along(slot, b, ay_send, other_y).wait_recv()
                    multiply(slot, b)

    def swap(b):
        return remote(
            acc.at[b, pl.ds(pl.multiple_of((1 - ci) * half, LANES), half), :],
            recv_c.at[b],
            csend.at[b],
            crecv.at[b],
            {"chan": 1 - ci},
        )

    def out_copy(q, b, source_slot):
        return remote(
            obuf.at[b, pl.ds(q * local_len, local_len), :],
            land.at[source_slot, b],
            osend.at[q, b],
            orecv.at[source_slot, b],
            {"ctx": ci * per + q, "chan": dest_chan},
        )

    def is_self(q):
        return jnp.logical_and(ci * per + q == me, dest_chan == ci)

    my_slot = lax.rem(me, per)

    def send_out(b):
        swap(b).wait()
        obuf[b] = (acc[b, mine, :] + recv_c[b]).astype(BF16)
        for q in range(per):

            @pl.when(jnp.logical_not(is_self(q)))
            def _():
                out_copy(q, b, my_slot).start()

            @pl.when(is_self(q))
            def _():
                land[my_slot, b] = obuf[b, q * local_len : (q + 1) * local_len, :]

    for b in range(genomes):
        for step in range(1, nz):
            if b == 0 or step == nz - 1:
                z_step(b, step)
            if step >= 2 and b + 1 < genomes:
                z_step(b + 1, step - 1)
        if b > 0:
            send_out(b - 1)
        y_step(b)
        swap(b).start()
    send_out(genomes - 1)

    for b in range(genomes):
        for q in range(per):

            @pl.when(jnp.logical_not(is_self(q)))
            def _():
                out_copy(q, b, q).wait_recv()

            out_ref[b, :, q * cols : (q + 1) * cols] = land[q, b]

    for off in range(1, ctx):
        remote(
            tok_ref, tok_all.at[me], tok_send.at[off], tok_recv.at[me], {"ctx": lax.rem(me + off, ctx)}
        ).wait_send()
    for h in range(pieces):
        for off in range(1, groups):
            group_copy(off, h, gi, lax.rem(gi + off, groups)).wait_send()
        for dz in range(nz):
            if ny == 2:
                y_copy(dz, h).wait_send()

            @pl.when(z < dz)
            def _():
                right_copy(dz, h).wait_send()

            @pl.when(z > dz)
            def _():
                left_copy(dz, h).wait_send()

    for b in range(genomes):
        for q in range(per):

            @pl.when(jnp.logical_not(is_self(q)))
            def _():
                out_copy(q, b, my_slot).wait_send()

        for dz in range(nz):
            slot = dz * ny + y

            @pl.when(jnp.logical_and(dz <= z, z < nz - 1))
            def _():
                along(slot, b, ar_send, right).wait_send()

            @pl.when(jnp.logical_and(dz >= z, z > 0))
            def _():
                along(slot, b, al_send, left).wait_send()

            if ny == 2:
                along(slot, b, ay_send, other_y).wait_send()


def body(
    groups,
    ctx,
    chans,
    tokens,
    embed_table,
    norm_gain,
    input_proj,
    short_filter,
    pole_rate,
    residue,
    skip_gain,
    output_proj,
):
    genomes, local_len = tokens.shape
    length = local_len * ctx
    features, branches, channels = input_proj.shape
    vocab = embed_table.shape[0]
    filter_count, poles = pole_rate.shape
    group_size = channels // filter_count
    share = channels // ctx
    filters = filter_count // ctx
    cols = output_proj.shape[1]
    rows = vocab // groups
    ny = 2 if ctx % 2 == 0 and ctx <= 8 else 1
    nz = ctx // ny
    taps = short_filter.shape[2]
    me = lax.axis_index("ctx")
    gi = lax.axis_index("groups")
    half = length // chans
    per = ctx // chans

    own_rows = lax.dynamic_slice_in_dim(embed_table, gi * rows, rows, 0)
    wide = own_rows.astype(F32)
    inv_rms = lax.rsqrt(jnp.mean(wide * wide, axis=-1, keepdims=True) + EPSILON)
    own_feats = lax.dynamic_slice_in_dim(own_rows, me * features, features, 1).astype(F32)
    gain = lax.dynamic_slice_in_dim(norm_gain, me * features, features, 0)
    normed = (own_feats * inv_rms * gain).astype(BF16)

    def padded(array):
        if share == LANES:
            return array
        cut = array.reshape(array.shape[:-1] + (ctx, share))
        pads = [(0, 0)] * (cut.ndim - 1) + [(0, LANES - share)]
        return jnp.pad(cut, pads).reshape(array.shape[:-1] + (ctx * LANES,))

    def own_share(array):
        wide_array = jnp.repeat(array, group_size, axis=-1)
        return jnp.pad(wide_array, [(0, 0)] * (array.ndim - 1) + [(0, LANES - share)])

    weights = padded(jnp.transpose(input_proj, (1, 0, 2)))
    out_weights = output_proj
    if share != LANES:
        out_weights = jnp.pad(
            output_proj.reshape(ctx, share, cols), ((0, 0), (0, LANES - share), (0, 0))
        ).reshape(ctx * LANES, cols)
    own_filter = lax.dynamic_slice_in_dim(short_filter, me * filters, filters, 1)
    tap_rows = own_share(jnp.transpose(own_filter, (0, 2, 1)).reshape(branches * taps, filters))
    rate = lax.dynamic_slice_in_dim(pole_rate, me * filters, filters, 0)
    own_residue = lax.dynamic_slice_in_dim(residue, me * filters, filters, 0)
    amp = own_residue * jnp.sqrt(-jnp.expm1(-2.0 * rate))
    skip = lax.dynamic_slice_in_dim(skip_gain, me * share, share, 0)
    skip = jnp.pad(skip, (0, LANES - share)).reshape(1, LANES)

    vmem = pl.BlockSpec(memory_space=pltpu.VMEM)
    dma = pltpu.SemaphoreType.DMA
    wide_lanes = 3 * LANES
    result = pl.pallas_call(
        functools.partial(kernel, (groups, ctx, chans, ny, group_size)),
        out_shape=jax.ShapeDtypeStruct((genomes, local_len, cols * per), BF16),
        in_specs=[vmem] * 8 + [pl.BlockSpec(memory_space=pl.ANY)],
        out_specs=vmem,
        scratch_shapes=[
            pltpu.VMEM((ctx, genomes, local_len), jnp.int32),
            pltpu.VMEM((genomes, length, LANES), jnp.int32),
            pltpu.VMEM((nz, PIECES, rows // PIECES, wide_lanes), BF16),
            pltpu.VMEM((nz, PIECES, rows // PIECES, wide_lanes), F32),
            pltpu.VMEM((nz, PIECES, rows // PIECES, wide_lanes), BF16),
            pltpu.VMEM((nz, PIECES, rows // PIECES, wide_lanes), BF16),
            pltpu.VMEM((nz, PIECES, rows // PIECES, wide_lanes), BF16),
            pltpu.VMEM((nz, PIECES, rows // PIECES, wide_lanes), BF16),
            pltpu.VMEM((groups, PIECES, rows // PIECES, wide_lanes), BF16),
            pltpu.VMEM((filters, LANES, length), BF16),
            pltpu.VMEM((length, LANES), F32),
            pltpu.VMEM((ctx, genomes, length, LANES), BF16),
            pltpu.VMEM((genomes, length, cols), F32),
            pltpu.VMEM((genomes, half, cols), F32),
            pltpu.VMEM((genomes, half, cols), BF16),
            pltpu.VMEM((per, genomes, local_len, cols), BF16),
            pltpu.VMEM((vocab, cols), BF16),
            dma((ctx,)),
            dma((ctx,)),
            dma((nz, PIECES)),
            dma((nz, PIECES)),
            dma((nz, PIECES)),
            dma((nz, PIECES)),
            dma((nz, PIECES)),
            dma((groups, PIECES)),
            dma((groups, PIECES)),
            dma((ctx, genomes)),
            dma((ctx, genomes)),
            dma((ctx, genomes)),
            dma((ctx, genomes)),
            dma((genomes,)),
            dma((genomes,)),
            dma((per, genomes)),
            dma((per, genomes)),
            dma((1,)),
        ],
        compiler_params=pltpu.CompilerParams(
            collective_id=0, has_side_effects=True, vmem_limit_bytes=50 * 1024 * 1024
        ),
    )(
        tokens,
        normed,
        weights,
        tap_rows,
        rate[:, :, None],
        amp[:, :, None],
        skip,
        out_weights,
        embed_table,
    )
    return result


def solution(mesh):
    sizes = mesh.shape
    return jax.shard_map(
        functools.partial(body, sizes["groups"], sizes["ctx"], sizes["chan"]),
        mesh=mesh,
        in_specs=(
            P("groups", "ctx"),
            P(),
            P(),
            P("ctx", None, "chan"),
            P(None, "chan", None),
            P("chan", None),
            P("chan", None),
            P("chan"),
            P("chan", "ctx"),
        ),
        out_specs=P("groups", "ctx", "chan"),
        check_vma=False,
    )
```

```python
import functools

import jax
import jax.numpy as jnp
from jax import lax
from jax.experimental import pallas as pl
from jax.experimental.pallas import tpu as pltpu
from jax.sharding import PartitionSpec as P

EPSILON = 1e-06
LANES = 128
PIECES = 4
MESH = pl.DeviceIdType.MESH
F32 = jnp.float32
BF16 = jnp.bfloat16


def remote(src, dst, send_sem, recv_sem, where):
    return pltpu.make_async_remote_copy(
        src_ref=src,
        dst_ref=dst,
        send_sem=send_sem,
        recv_sem=recv_sem,
        device_id=where,
        device_id_type=MESH,
    )


def kernel(
    sizes,
    tok_hbm,
    gain_hbm,
    w_hbm,
    taps_hbm,
    rate_hbm,
    residue_hbm,
    skip_hbm,
    wout_hbm,
    table_ref,
    out_ref,
    tok_ref,
    gain_ref,
    w_ref,
    short_ref,
    rate_ref,
    residue_ref,
    skip_ref,
    wout_ref,
    own_rows,
    norm_ref,
    taps_ref,
    tok_all,
    tok_col,
    part_y,
    part_own,
    recv_y,
    recv_r,
    recv_l,
    sum_z,
    vocab_proj,
    toeplitz,
    conv,
    gathered,
    acc,
    recv_c,
    obuf,
    land,
    table_cols,
    tok_send,
    tok_recv,
    ysend,
    yrecv,
    zsend,
    rrecv,
    lrecv,
    gsend,
    grecv,
    ar_send,
    al_send,
    ay_send,
    arecv,
    csend,
    crecv,
    osend,
    orecv,
    local_sem,
):
    groups, ctx, chans, ny, group_size, filters = sizes
    nz = ctx // ny
    genomes, local_len = tok_ref.shape
    length = local_len * ctx
    rows, features = norm_ref.shape
    width_all = own_rows.shape[1]
    vocab = rows * groups
    cols = wout_ref.shape[1]
    poles, filters_all = rate_ref.shape
    half = length // chans
    per = ctx // chans

    gi = lax.axis_index("groups")
    me = lax.axis_index("ctx")
    ci = lax.axis_index("chan")
    y = lax.rem(me, ny)
    z = me // ny
    other_y = z * ny + (ny - 1 - y)
    right, left = me + ny, me - ny
    dest_chan = me // per

    barrier = pltpu.get_barrier_semaphore()

    def greet(where):
        pl.semaphore_signal(barrier, inc=1, device_id=where, device_id_type=MESH)

    for off in range(1, ctx):
        greet({"ctx": lax.rem(me + off, ctx)})
    for off in range(1, groups):
        greet({"groups": lax.rem(gi + off, groups)})
    greet({"chan": 1 - ci})
    for q in range(per):
        target = ci * per + q

        @pl.when(jnp.logical_or(target != me, dest_chan != ci))
        def _():
            greet({"ctx": target, "chan": dest_chan})

    def lane_block(ref, index, size):
        return ref.at[:, pl.ds(pl.multiple_of(index * size, LANES), size)]

    loads = [
        (table_ref.at[pl.ds(pl.multiple_of(gi * rows, 16), rows), :], own_rows),
        (lane_block(gain_hbm, me, features), gain_ref),
        (w_hbm, w_ref),
        (tok_hbm, tok_ref),
        (taps_hbm, short_ref),
        (rate_hbm, rate_ref),
        (residue_hbm, residue_ref),
        (lane_block(skip_hbm, me, LANES), skip_ref),
        (wout_hbm, wout_ref),
        (lane_block(table_ref, me, cols), table_cols),
    ]
    copies = [
        pltpu.make_async_copy(source, target, local_sem.at[n])
        for n, (source, target) in enumerate(loads)
    ]
    for copy in copies:
        copy.start()

    copies[0].wait()
    copies[1].wait()
    squares = jnp.zeros((rows, LANES), F32)
    for at in range(0, width_all, LANES):
        wide = own_rows[:, at : at + LANES].astype(F32)
        squares = squares + wide * wide
    inv_rms = lax.rsqrt(jnp.sum(squares, axis=1, keepdims=True) / width_all + EPSILON)
    feats = own_rows[:, pl.ds(pl.multiple_of(me * features, LANES), features)].astype(F32)
    norm_ref[...] = (feats * inv_rms * gain_ref[...]).astype(BF16)
    copies[3].wait()
    copies[2].wait()

    self_target = jnp.where(dest_chan == ci, 1, 0)
    pl.semaphore_wait(barrier, ctx - 1 + groups - 1 + 1 + per - self_target)

    tok_all[me] = tok_ref[...]
    for off in range(1, ctx):
        peer = lax.rem(me + off, ctx)
        remote(
            tok_ref, tok_all.at[me], tok_send.at[off], tok_recv.at[me], {"ctx": peer}
        ).start()

    pieces = part_own.shape[1]
    piece = rows // pieces

    order = []
    for step in range((nz + 1) // 2):
        order.append(nz - 1 - step)
        if step != nz - 1 - step:
            order.append(step)

    def y_copy(dz, h):
        return remote(
            part_y.at[dz, h], recv_y.at[dz, h], ysend.at[dz, h], yrecv.at[dz, h], {"ctx": other_y}
        )

    for dz in order:
        for branch in range(3):
            lanes = slice(branch * LANES, (branch + 1) * LANES)
            both = jnp.dot(
                norm_ref[...],
                w_ref[branch, :, dz * ny * LANES : (dz + 1) * ny * LANES],
                preferred_element_type=F32,
            )
            keep = both
            if ny == 2:
                first, second = both[:, :LANES], both[:, LANES:]
                keep = jnp.where(y == 0, first, second)
                give = jnp.where(y == 0, second, first).astype(BF16)
            for h in range(pieces):
                part_own[dz, h, :, lanes] = keep[h * piece : (h + 1) * piece]
                if ny == 2:
                    part_y[dz, h, :, lanes] = give[h * piece : (h + 1) * piece]
        if ny == 2:
            y_copy(dz, 0).start()
    if ny == 2:
        for h in range(1, pieces):
            for dz in order:
                y_copy(dz, h).start()

    def with_y(dz, h):
        value = part_own[dz, h]
        if ny == 2:
            y_copy(dz, h).wait_recv()
            value = value + recv_y[dz, h].astype(F32)
        return value

    def right_copy(dz, h):
        return remote(
            sum_z.at[dz, h], recv_r.at[dz, h], zsend.at[dz, h], rrecv.at[dz, h], {"ctx": right}
        )

    def left_copy(dz, h):
        return remote(
            sum_z.at[dz, h], recv_l.at[dz, h], zsend.at[dz, h], lrecv.at[dz, h], {"ctx": left}
        )

    def sum_step(h, step):
        dr, dl = nz - 1 - step, step

        @pl.when(z < dr)
        def _():
            part_own[dr, h] = with_y(dr, h)

            @pl.when(z > 0)
            def _():
                right_copy(dr, h).wait_recv()
                part_own[dr, h] = part_own[dr, h] + recv_r[dr, h].astype(F32)

            sum_z[dr, h] = part_own[dr, h].astype(BF16)
            right_copy(dr, h).start()

        @pl.when(z > dl)
        def _():
            part_own[dl, h] = with_y(dl, h)

            @pl.when(z < nz - 1)
            def _():
                left_copy(dl, h).wait_recv()
                part_own[dl, h] = part_own[dl, h] + recv_l[dl, h].astype(F32)

            sum_z[dl, h] = part_own[dl, h].astype(BF16)
            left_copy(dl, h).start()

    def group_copy(off, h, source, peer):
        return remote(
            vocab_proj.at[source, h],
            vocab_proj.at[source, h],
            gsend.at[off, h],
            grecv.at[source, h],
            {"groups": peer},
        )

    def finish(h):
        part_own[z, h] = with_y(z, h)

        @pl.when(z > 0)
        def _():
            right_copy(z, h).wait_recv()
            part_own[z, h] = part_own[z, h] + recv_r[z, h].astype(F32)

        @pl.when(z < nz - 1)
        def _():
            left_copy(z, h).wait_recv()
            part_own[z, h] = part_own[z, h] + recv_l[z, h].astype(F32)

        vocab_proj[gi, h] = part_own[z, h].astype(BF16)
        for off in range(1, groups):
            group_copy(off, h, gi, lax.rem(gi + off, groups)).start()

    width = length + LANES
    lag = length - 1 - lax.broadcasted_iota(jnp.int32, (poles, width), 1)
    lag_f = jnp.maximum(lag, 0).astype(F32)

    for copy in copies[4:8]:
        copy.wait()
    doubled = -2.0 * rate_ref[...]
    decayed = jnp.exp(doubled)
    pole_amp = residue_ref[...] * jnp.sqrt((1.0 - decayed) * doubled / jnp.log(decayed))
    filter_ids = lax.broadcasted_iota(jnp.int32, (poles, filters_all), 1)
    lane_ids = lax.broadcasted_iota(jnp.int32, (filters_all, LANES), 1)
    spread_ids = lane_ids // group_size
    chosen = jnp.logical_and(
        spread_ids < filters,
        spread_ids + me * filters == lax.broadcasted_iota(jnp.int32, (filters_all, LANES), 0),
    )
    spread = jnp.where(chosen, 1.0, 0.0)
    for branch in range(3):
        taps_ref[branch * 3 : (branch + 1) * 3, :] = jnp.dot(
            short_ref[branch], spread, precision=lax.Precision.HIGHEST, preferred_element_type=F32
        )

    def long_filter(f):
        here = filter_ids == me * filters + f
        rate = jnp.sum(jnp.where(here, rate_ref[...], 0.0), axis=1, keepdims=True)
        amp = jnp.sum(jnp.where(here, pole_amp, 0.0), axis=1, keepdims=True)
        taps = jnp.sum(amp * jnp.exp(-rate * lag_f), axis=0, keepdims=True)
        taps = jnp.where(lag[:1] >= 0, taps, 0.0)
        rolled = pltpu.roll(
            jnp.broadcast_to(taps, (LANES, width)), width - (LANES - 1), 1, stride=1, stride_axis=0
        )
        toeplitz[f] = rolled[:, :length].astype(BF16)

    steps = []
    for h in range(pieces):
        for step in range(nz - 1):
            steps.append((sum_step, (h, step)))
            if step == 0 and h > 0:
                steps.append((finish, (h - 1,)))
    waiting = list(range(filters))
    for action, arguments in steps:
        action(*arguments)
        for f in waiting[:2]:
            long_filter(f)
        waiting = waiting[2:]
    for f in waiting:
        long_filter(f)

    for off in range(1, ctx):
        peer = lax.rem(me + off, ctx)
        remote(
            tok_ref, tok_all.at[peer], tok_send.at[off], tok_recv.at[peer], {"ctx": peer}
        ).wait_recv()
    for b in range(genomes):
        line = jnp.concatenate([tok_all[i, b : b + 1, :] for i in range(ctx)], axis=1)
        tok_col[b] = jnp.transpose(jnp.broadcast_to(line, (LANES, length)))

    finish(pieces - 1)
    for h in range(pieces):
        for off in range(1, groups):
            peer = lax.rem(gi + off, groups)
            group_copy(off, h, peer, peer).wait_recv()

    table_proj = vocab_proj[...].reshape(vocab, 3 * LANES)

    def onehot(columns):
        parts = []
        for v in range(vocab // LANES):
            ids = lax.broadcasted_iota(jnp.int32, columns.shape, 1) + v * LANES
            parts.append(jnp.where(columns == ids, 1.0, 0.0).astype(BF16))
        return jnp.concatenate(parts, axis=1)

    row_ids = lax.broadcasted_iota(jnp.int32, (length, LANES), 0)
    lane_filter = lax.broadcasted_iota(jnp.int32, (length, LANES), 1) // group_size
    blocks = length // LANES

    def along(slot, b, sems, where):
        return remote(
            gathered.at[slot, b],
            gathered.at[slot, b],
            sems.at[slot, b],
            arecv.at[slot, b],
            {"ctx": where},
        )

    for b in range(genomes):
        projected = jnp.dot(onehot(tok_col[b]), table_proj, preferred_element_type=F32)
        filtered = []
        for branch in range(3):
            value = projected[:, branch * LANES : (branch + 1) * LANES]
            total = taps_ref[branch * 3 : branch * 3 + 1, :] * value
            for k in (1, 2):
                shifted = jnp.where(row_ids >= k, pltpu.roll(value, k, 0), 0.0)
                at = branch * 3 + k
                total = total + taps_ref[at : at + 1, :] * shifted
            filtered.append(total)
        product = filtered[1] * filtered[2]
        for f in range(filters):
            masked = jnp.where(lane_filter == f, product, 0.0).astype(BF16)
            for i in range(blocks):
                term = jnp.dot(
                    toeplitz[f, :, (blocks - 1 - i) * LANES :],
                    masked[: (i + 1) * LANES],
                    preferred_element_type=F32,
                )
                at = slice(i * LANES, (i + 1) * LANES)
                conv[at, :] = term if f == 0 else conv[at, :] + term
        gated = filtered[0] * (conv[...] + skip_ref[...] * product)
        gathered[me, b] = gated.astype(BF16)

        @pl.when(z < nz - 1)
        def _():
            along(me, b, ar_send, right).start()

        @pl.when(z > 0)
        def _():
            along(me, b, al_send, left).start()

        if ny == 2:
            along(me, b, ay_send, other_y).start()

    def block_product(slot, b):
        weight = wout_ref[pl.ds(pl.multiple_of(slot * LANES, LANES), LANES), :]
        return jnp.dot(gathered[slot, b], weight, preferred_element_type=F32)

    mine = pl.ds(pl.multiple_of(ci * half, LANES), half)
    copies[8].wait()
    copies[9].wait()
    for b in range(genomes):
        acc[b] = block_product(me, b)
        acc[b, mine, :] = acc[b, mine, :] + jnp.dot(
            onehot(tok_col[b, mine, :]), table_cols[...], preferred_element_type=F32
        )

    def multiply(slot, b):
        acc[b] = acc[b] + block_product(slot, b)

    def z_step(b, step):
        from_left = me - step * ny
        from_right = me + step * ny

        @pl.when(from_left >= 0)
        def _():
            along(from_left, b, ar_send, right).wait_recv()

            @pl.when(z < nz - 1)
            def _():
                along(from_left, b, ar_send, right).start()

            if ny == 2:
                along(from_left, b, ay_send, other_y).start()

        @pl.when(from_right < ctx)
        def _():
            along(from_right, b, al_send, left).wait_recv()

            @pl.when(z > 0)
            def _():
                along(from_right, b, al_send, left).start()

            if ny == 2:
                along(from_right, b, ay_send, other_y).start()

        @pl.when(from_left >= 0)
        def _():
            multiply(from_left, b)

        @pl.when(from_right < ctx)
        def _():
            multiply(from_right, b)

    def y_step(b):
        if ny == 1:
            return
        for step in range(nz):
            for toward in (-1, 1) if step > 0 else (1,):
                twin_z = z + toward * step

                @pl.when(jnp.logical_and(twin_z >= 0, twin_z < nz))
                def _():
                    slot = twin_z * ny + (1 - y)
                    along(slot, b, ay_send, other_y).wait_recv()
                    multiply(slot, b)

    def swap(b):
        return remote(
            acc.at[b, pl.ds(pl.multiple_of((1 - ci) * half, LANES), half), :],
            recv_c.at[b],
            csend.at[b],
            crecv.at[b],
            {"chan": 1 - ci},
        )

    def out_copy(q, b, source_slot):
        return remote(
            obuf.at[b, pl.ds(q * local_len, local_len), :],
            land.at[source_slot, b],
            osend.at[q, b],
            orecv.at[source_slot, b],
            {"ctx": ci * per + q, "chan": dest_chan},
        )

    def is_self(q):
        return jnp.logical_and(ci * per + q == me, dest_chan == ci)

    my_slot = lax.rem(me, per)

    def send_out(b):
        swap(b).wait()
        obuf[b] = (acc[b, mine, :] + recv_c[b]).astype(BF16)
        for q in range(per):

            @pl.when(jnp.logical_not(is_self(q)))
            def _():
                out_copy(q, b, my_slot).start()

            @pl.when(is_self(q))
            def _():
                land[my_slot, b] = obuf[b, q * local_len : (q + 1) * local_len, :]

    for b in range(genomes):
        for step in range(1, nz):
            if b == 0 or step == nz - 1:
                z_step(b, step)
            if step >= 2 and b + 1 < genomes:
                z_step(b + 1, step - 1)
        if b > 0:
            send_out(b - 1)
        y_step(b)
        swap(b).start()
    send_out(genomes - 1)

    for b in range(genomes):
        for q in range(per):

            @pl.when(jnp.logical_not(is_self(q)))
            def _():
                out_copy(q, b, q).wait_recv()

            out_ref[b, :, q * cols : (q + 1) * cols] = land[q, b]

    for off in range(1, ctx):
        remote(
            tok_ref, tok_all.at[me], tok_send.at[off], tok_recv.at[me], {"ctx": lax.rem(me + off, ctx)}
        ).wait_send()
    for h in range(pieces):
        for off in range(1, groups):
            group_copy(off, h, gi, lax.rem(gi + off, groups)).wait_send()
        for dz in range(nz):
            if ny == 2:
                y_copy(dz, h).wait_send()

            @pl.when(z < dz)
            def _():
                right_copy(dz, h).wait_send()

            @pl.when(z > dz)
            def _():
                left_copy(dz, h).wait_send()

    for b in range(genomes):
        for q in range(per):

            @pl.when(jnp.logical_not(is_self(q)))
            def _():
                out_copy(q, b, my_slot).wait_send()

        for dz in range(nz):
            slot = dz * ny + y

            @pl.when(jnp.logical_and(dz <= z, z < nz - 1))
            def _():
                along(slot, b, ar_send, right).wait_send()

            @pl.when(jnp.logical_and(dz >= z, z > 0))
            def _():
                along(slot, b, al_send, left).wait_send()

            if ny == 2:
                along(slot, b, ay_send, other_y).wait_send()


def body(
    groups,
    ctx,
    chans,
    tokens,
    embed_table,
    norm_gain,
    input_proj,
    short_filter,
    pole_rate,
    residue,
    skip_gain,
    output_proj,
):
    genomes, local_len = tokens.shape
    length = local_len * ctx
    features, branches, channels = input_proj.shape
    vocab = embed_table.shape[0]
    filter_count, poles = pole_rate.shape
    group_size = channels // filter_count
    share = channels // ctx
    filters = filter_count // ctx
    cols = output_proj.shape[1]
    rows = vocab // groups
    ny = 2 if ctx % 2 == 0 and ctx <= 8 else 1
    nz = ctx // ny
    taps = short_filter.shape[2]
    half = length // chans
    per = ctx // chans

    def padded(array):
        if share == LANES:
            return array
        cut = array.reshape(array.shape[:-1] + (ctx, share))
        pads = [(0, 0)] * (cut.ndim - 1) + [(0, LANES - share)]
        return jnp.pad(cut, pads).reshape(array.shape[:-1] + (ctx * LANES,))

    weights = padded(jnp.transpose(input_proj, (1, 0, 2)))
    out_weights = output_proj
    if share != LANES:
        out_weights = jnp.pad(
            output_proj.reshape(ctx, share, cols), ((0, 0), (0, LANES - share), (0, 0))
        ).reshape(ctx * LANES, cols)
    short = jnp.transpose(short_filter, (0, 2, 1))
    skip = padded(skip_gain).reshape(1, ctx * LANES)

    vmem = pl.BlockSpec(memory_space=pltpu.VMEM)
    dma = pltpu.SemaphoreType.DMA
    wide_lanes = 3 * LANES
    result = pl.pallas_call(
        functools.partial(kernel, (groups, ctx, chans, ny, group_size, filters)),
        out_shape=jax.ShapeDtypeStruct((genomes, local_len, cols * per), BF16),
        in_specs=[pl.BlockSpec(memory_space=pl.ANY)] * 9,
        out_specs=vmem,
        scratch_shapes=[
            pltpu.VMEM((genomes, local_len), jnp.int32),
            pltpu.VMEM((1, features), F32),
            pltpu.VMEM((branches, features, ctx * LANES), BF16),
            pltpu.VMEM((branches, taps, filter_count), F32),
            pltpu.VMEM((poles, filter_count), F32),
            pltpu.VMEM((poles, filter_count), F32),
            pltpu.VMEM((1, LANES), F32),
            pltpu.VMEM((ctx * LANES, cols), BF16),
            pltpu.VMEM((rows, features * ctx), BF16),
            pltpu.VMEM((rows, features), BF16),
            pltpu.VMEM((branches * taps, LANES), F32),
            pltpu.VMEM((ctx, genomes, local_len), jnp.int32),
            pltpu.VMEM((genomes, length, LANES), jnp.int32),
            pltpu.VMEM((nz, PIECES, rows // PIECES, wide_lanes), BF16),
            pltpu.VMEM((nz, PIECES, rows // PIECES, wide_lanes), F32),
            pltpu.VMEM((nz, PIECES, rows // PIECES, wide_lanes), BF16),
            pltpu.VMEM((nz, PIECES, rows // PIECES, wide_lanes), BF16),
            pltpu.VMEM((nz, PIECES, rows // PIECES, wide_lanes), BF16),
            pltpu.VMEM((nz, PIECES, rows // PIECES, wide_lanes), BF16),
            pltpu.VMEM((groups, PIECES, rows // PIECES, wide_lanes), BF16),
            pltpu.VMEM((filters, LANES, length), BF16),
            pltpu.VMEM((length, LANES), F32),
            pltpu.VMEM((ctx, genomes, length, LANES), BF16),
            pltpu.VMEM((genomes, length, cols), F32),
            pltpu.VMEM((genomes, half, cols), F32),
            pltpu.VMEM((genomes, half, cols), BF16),
            pltpu.VMEM((per, genomes, local_len, cols), BF16),
            pltpu.VMEM((vocab, cols), BF16),
            dma((ctx,)),
            dma((ctx,)),
            dma((nz, PIECES)),
            dma((nz, PIECES)),
            dma((nz, PIECES)),
            dma((nz, PIECES)),
            dma((nz, PIECES)),
            dma((groups, PIECES)),
            dma((groups, PIECES)),
            dma((ctx, genomes)),
            dma((ctx, genomes)),
            dma((ctx, genomes)),
            dma((ctx, genomes)),
            dma((genomes,)),
            dma((genomes,)),
            dma((per, genomes)),
            dma((per, genomes)),
            dma((10,)),
        ],
        compiler_params=pltpu.CompilerParams(
            collective_id=0, has_side_effects=True, vmem_limit_bytes=56 * 1024 * 1024
        ),
    )(
        tokens,
        norm_gain.reshape(1, features * ctx),
        weights,
        short,
        jnp.transpose(pole_rate),
        jnp.transpose(residue),
        skip,
        out_weights,
        embed_table,
    )
    return result


def solution(mesh):
    sizes = mesh.shape
    return jax.shard_map(
        functools.partial(body, sizes["groups"], sizes["ctx"], sizes["chan"]),
        mesh=mesh,
        in_specs=(
            P("groups", "ctx"),
            P(),
            P(),
            P("ctx", None, "chan"),
            P(None, "chan", None),
            P("chan", None),
            P("chan", None),
            P("chan"),
            P("chan", "ctx"),
        ),
        out_specs=P("groups", "ctx", "chan"),
        check_vma=False,
    )
```

```python
import functools

import jax
import jax.numpy as jnp
from jax import lax
from jax.experimental import pallas as pl
from jax.experimental.pallas import tpu as pltpu
from jax.sharding import PartitionSpec as P

EPSILON = 1e-06
LANES = 128
PIECES = 2
MESH = pl.DeviceIdType.MESH
F32 = jnp.float32
BF16 = jnp.bfloat16


def remote(src, dst, send_sem, recv_sem, where):
    return pltpu.make_async_remote_copy(
        src_ref=src,
        dst_ref=dst,
        send_sem=send_sem,
        recv_sem=recv_sem,
        device_id=where,
        device_id_type=MESH,
    )


def kernel(
    sizes,
    tok_hbm,
    gain_hbm,
    w_hbm,
    taps_hbm,
    rate_hbm,
    residue_hbm,
    skip_hbm,
    wout_hbm,
    table_ref,
    out_ref,
    tok_ref,
    gain_ref,
    w_ref,
    short_ref,
    rate_ref,
    residue_ref,
    skip_ref,
    wout_ref,
    own_rows,
    norm_ref,
    taps_ref,
    tok_all,
    tok_col,
    part_y,
    part_own,
    recv_y,
    recv_r,
    recv_l,
    sum_z,
    vocab_proj,
    toeplitz,
    conv,
    gathered,
    acc,
    recv_c,
    obuf,
    land,
    table_cols,
    tok_send,
    tok_recv,
    ysend,
    yrecv,
    zsend,
    rrecv,
    lrecv,
    gsend,
    grecv,
    ar_send,
    al_send,
    ay_send,
    arecv,
    csend,
    crecv,
    osend,
    orecv,
    local_sem,
):
    groups, ctx, chans, ny, group_size, filters = sizes
    nz = ctx // ny
    genomes, local_len = tok_ref.shape
    length = local_len * ctx
    rows, features = norm_ref.shape
    width_all = own_rows.shape[1]
    vocab = rows * groups
    cols = wout_ref.shape[1]
    poles, filters_all = rate_ref.shape
    half = length // chans
    per = ctx // chans

    gi = lax.axis_index("groups")
    me = lax.axis_index("ctx")
    ci = lax.axis_index("chan")
    y = lax.rem(me, ny)
    z = me // ny
    other_y = z * ny + (ny - 1 - y)
    right, left = me + ny, me - ny
    dest_chan = me // per

    barrier = pltpu.get_barrier_semaphore()

    def greet(where):
        pl.semaphore_signal(barrier, inc=1, device_id=where, device_id_type=MESH)

    for off in range(1, ctx):
        greet({"ctx": lax.rem(me + off, ctx)})
    for off in range(1, groups):
        greet({"groups": lax.rem(gi + off, groups)})
    greet({"chan": 1 - ci})
    for q in range(per):
        target = ci * per + q

        @pl.when(jnp.logical_or(target != me, dest_chan != ci))
        def _():
            greet({"ctx": target, "chan": dest_chan})

    def lane_block(ref, index, size):
        return ref.at[:, pl.ds(pl.multiple_of(index * size, LANES), size)]

    loads = [
        (table_ref.at[pl.ds(pl.multiple_of(gi * rows, 16), rows), :], own_rows),
        (lane_block(gain_hbm, me, features), gain_ref),
        (w_hbm, w_ref),
        (tok_hbm, tok_ref),
        (taps_hbm, short_ref),
        (rate_hbm, rate_ref),
        (residue_hbm, residue_ref),
        (lane_block(skip_hbm, me, LANES), skip_ref),
        (wout_hbm, wout_ref),
        (lane_block(table_ref, me, cols), table_cols),
    ]
    copies = [
        pltpu.make_async_copy(source, target, local_sem.at[n])
        for n, (source, target) in enumerate(loads)
    ]
    for copy in copies:
        copy.start()

    copies[0].wait()
    copies[1].wait()
    squares = jnp.zeros((rows, LANES), F32)
    for at in range(0, width_all, LANES):
        wide = own_rows[:, at : at + LANES].astype(F32)
        squares = squares + wide * wide
    inv_rms = lax.rsqrt(jnp.sum(squares, axis=1, keepdims=True) / width_all + EPSILON)
    feats = own_rows[:, pl.ds(pl.multiple_of(me * features, LANES), features)].astype(F32)
    norm_ref[...] = (feats * inv_rms * gain_ref[...]).astype(BF16)
    copies[3].wait()
    copies[2].wait()

    self_target = jnp.where(dest_chan == ci, 1, 0)
    pl.semaphore_wait(barrier, ctx - 1 + groups - 1 + 1 + per - self_target)

    tok_all[me] = tok_ref[...]
    for off in range(1, ctx):
        peer = lax.rem(me + off, ctx)
        remote(
            tok_ref, tok_all.at[me], tok_send.at[off], tok_recv.at[me], {"ctx": peer}
        ).start()

    pieces = part_own.shape[1]
    piece = rows // pieces

    order = []
    for step in range((nz + 1) // 2):
        order.append(nz - 1 - step)
        if step != nz - 1 - step:
            order.append(step)

    def y_copy(dz, h):
        return remote(
            part_y.at[dz, h], recv_y.at[dz, h], ysend.at[dz, h], yrecv.at[dz, h], {"ctx": other_y}
        )

    for dz in order:
        for branch in range(3):
            lanes = slice(branch * LANES, (branch + 1) * LANES)
            both = jnp.dot(
                norm_ref[...],
                w_ref[branch, :, dz * ny * LANES : (dz + 1) * ny * LANES],
                preferred_element_type=F32,
            )
            keep = both
            if ny == 2:
                first, second = both[:, :LANES], both[:, LANES:]
                keep = jnp.where(y == 0, first, second)
                give = jnp.where(y == 0, second, first).astype(BF16)
            for h in range(pieces):
                part_own[dz, h, :, lanes] = keep[h * piece : (h + 1) * piece]
                if ny == 2:
                    part_y[dz, h, :, lanes] = give[h * piece : (h + 1) * piece]
        if ny == 2:
            y_copy(dz, 0).start()
    if ny == 2:
        for h in range(1, pieces):
            for dz in order:
                y_copy(dz, h).start()

    def with_y(dz, h):
        value = part_own[dz, h]
        if ny == 2:
            y_copy(dz, h).wait_recv()
            value = value + recv_y[dz, h].astype(F32)
        return value

    def right_copy(dz, h):
        return remote(
            sum_z.at[dz, h], recv_r.at[dz, h], zsend.at[dz, h], rrecv.at[dz, h], {"ctx": right}
        )

    def left_copy(dz, h):
        return remote(
            sum_z.at[dz, h], recv_l.at[dz, h], zsend.at[dz, h], lrecv.at[dz, h], {"ctx": left}
        )

    def sum_step(h, step):
        dr, dl = nz - 1 - step, step

        @pl.when(z < dr)
        def _():
            part_own[dr, h] = with_y(dr, h)

            @pl.when(z > 0)
            def _():
                right_copy(dr, h).wait_recv()
                part_own[dr, h] = part_own[dr, h] + recv_r[dr, h].astype(F32)

            sum_z[dr, h] = part_own[dr, h].astype(BF16)
            right_copy(dr, h).start()

        @pl.when(z > dl)
        def _():
            part_own[dl, h] = with_y(dl, h)

            @pl.when(z < nz - 1)
            def _():
                left_copy(dl, h).wait_recv()
                part_own[dl, h] = part_own[dl, h] + recv_l[dl, h].astype(F32)

            sum_z[dl, h] = part_own[dl, h].astype(BF16)
            left_copy(dl, h).start()

    def group_copy(off, h, source, peer):
        return remote(
            vocab_proj.at[source, h],
            vocab_proj.at[source, h],
            gsend.at[off, h],
            grecv.at[source, h],
            {"groups": peer},
        )

    def finish(h):
        part_own[z, h] = with_y(z, h)

        @pl.when(z > 0)
        def _():
            right_copy(z, h).wait_recv()
            part_own[z, h] = part_own[z, h] + recv_r[z, h].astype(F32)

        @pl.when(z < nz - 1)
        def _():
            left_copy(z, h).wait_recv()
            part_own[z, h] = part_own[z, h] + recv_l[z, h].astype(F32)

        vocab_proj[gi, h] = part_own[z, h].astype(BF16)
        for off in range(1, groups):
            group_copy(off, h, gi, lax.rem(gi + off, groups)).start()

    width = length + LANES
    lag = length - 1 - lax.broadcasted_iota(jnp.int32, (poles, width), 1)
    lag_f = jnp.maximum(lag, 0).astype(F32)

    for copy in copies[4:8]:
        copy.wait()
    doubled = -2.0 * rate_ref[...]
    decayed = jnp.exp(doubled)
    pole_amp = residue_ref[...] * jnp.sqrt((1.0 - decayed) * doubled / jnp.log(decayed))
    filter_ids = lax.broadcasted_iota(jnp.int32, (poles, filters_all), 1)
    lane_ids = lax.broadcasted_iota(jnp.int32, (filters_all, LANES), 1)
    spread_ids = lane_ids // group_size
    chosen = jnp.logical_and(
        spread_ids < filters,
        spread_ids + me * filters == lax.broadcasted_iota(jnp.int32, (filters_all, LANES), 0),
    )
    spread = jnp.where(chosen, 1.0, 0.0)
    for branch in range(3):
        taps_ref[branch * 3 : (branch + 1) * 3, :] = jnp.dot(
            short_ref[branch], spread, precision=lax.Precision.HIGHEST, preferred_element_type=F32
        )

    def long_filter(f):
        here = filter_ids == me * filters + f
        rate = jnp.sum(jnp.where(here, rate_ref[...], 0.0), axis=1, keepdims=True)
        amp = jnp.sum(jnp.where(here, pole_amp, 0.0), axis=1, keepdims=True)
        taps = jnp.sum(amp * jnp.exp(-rate * lag_f), axis=0, keepdims=True)
        taps = jnp.where(lag[:1] >= 0, taps, 0.0)
        rolled = pltpu.roll(
            jnp.broadcast_to(taps, (LANES, width)), width - (LANES - 1), 1, stride=1, stride_axis=0
        )
        toeplitz[f] = rolled[:, :length].astype(BF16)

    steps = []
    for h in range(pieces):
        for step in range(nz - 1):
            steps.append((sum_step, (h, step)))
            if step == 0 and h > 0:
                steps.append((finish, (h - 1,)))
    waiting = list(range(filters))
    for action, arguments in steps:
        action(*arguments)
        for f in waiting[:2]:
            long_filter(f)
        waiting = waiting[2:]
    for f in waiting:
        long_filter(f)

    for off in range(1, ctx):
        peer = lax.rem(me + off, ctx)
        remote(
            tok_ref, tok_all.at[peer], tok_send.at[off], tok_recv.at[peer], {"ctx": peer}
        ).wait_recv()
    for b in range(genomes):
        line = jnp.concatenate([tok_all[i, b : b + 1, :] for i in range(ctx)], axis=1)
        tok_col[b] = jnp.transpose(jnp.broadcast_to(line, (LANES, length)))

    finish(pieces - 1)
    for h in range(pieces):
        for off in range(1, groups):
            peer = lax.rem(gi + off, groups)
            group_copy(off, h, peer, peer).wait_recv()

    table_proj = vocab_proj[...].reshape(vocab, 3 * LANES)

    def onehot(columns):
        parts = []
        for v in range(vocab // LANES):
            ids = lax.broadcasted_iota(jnp.int32, columns.shape, 1) + v * LANES
            parts.append(jnp.where(columns == ids, 1.0, 0.0).astype(BF16))
        return jnp.concatenate(parts, axis=1)

    row_ids = lax.broadcasted_iota(jnp.int32, (length, LANES), 0)
    lane_filter = lax.broadcasted_iota(jnp.int32, (length, LANES), 1) // group_size
    blocks = length // LANES

    def along(slot, b, sems, where):
        return remote(
            gathered.at[slot, b],
            gathered.at[slot, b],
            sems.at[slot, b],
            arecv.at[slot, b],
            {"ctx": where},
        )

    for b in range(genomes):
        projected = jnp.dot(onehot(tok_col[b]), table_proj, preferred_element_type=F32)
        filtered = []
        for branch in range(3):
            value = projected[:, branch * LANES : (branch + 1) * LANES]
            total = taps_ref[branch * 3 : branch * 3 + 1, :] * value
            for k in (1, 2):
                shifted = jnp.where(row_ids >= k, pltpu.roll(value, k, 0), 0.0)
                at = branch * 3 + k
                total = total + taps_ref[at : at + 1, :] * shifted
            filtered.append(total)
        product = filtered[1] * filtered[2]
        for f in range(filters):
            masked = jnp.where(lane_filter == f, product, 0.0).astype(BF16)
            for i in range(blocks):
                term = jnp.dot(
                    toeplitz[f, :, (blocks - 1 - i) * LANES :],
                    masked[: (i + 1) * LANES],
                    preferred_element_type=F32,
                )
                at = slice(i * LANES, (i + 1) * LANES)
                conv[at, :] = term if f == 0 else conv[at, :] + term
        gated = filtered[0] * (conv[...] + skip_ref[...] * product)
        gathered[me, b] = gated.astype(BF16)

        @pl.when(z < nz - 1)
        def _():
            along(me, b, ar_send, right).start()

        @pl.when(z > 0)
        def _():
            along(me, b, al_send, left).start()

        if ny == 2:
            along(me, b, ay_send, other_y).start()

    def block_product(slot, b):
        weight = wout_ref[pl.ds(pl.multiple_of(slot * LANES, LANES), LANES), :]
        return jnp.dot(gathered[slot, b], weight, preferred_element_type=F32)

    mine = pl.ds(pl.multiple_of(ci * half, LANES), half)
    copies[8].wait()
    copies[9].wait()
    for b in range(genomes):
        acc[b] = block_product(me, b)
        acc[b, mine, :] = acc[b, mine, :] + jnp.dot(
            onehot(tok_col[b, mine, :]), table_cols[...], preferred_element_type=F32
        )

    def multiply(slot, b):
        acc[b] = acc[b] + block_product(slot, b)

    def z_step(b, step):
        from_left = me - step * ny
        from_right = me + step * ny

        @pl.when(from_left >= 0)
        def _():
            along(from_left, b, ar_send, right).wait_recv()

            @pl.when(z < nz - 1)
            def _():
                along(from_left, b, ar_send, right).start()

            if ny == 2:
                along(from_left, b, ay_send, other_y).start()

        @pl.when(from_right < ctx)
        def _():
            along(from_right, b, al_send, left).wait_recv()

            @pl.when(z > 0)
            def _():
                along(from_right, b, al_send, left).start()

            if ny == 2:
                along(from_right, b, ay_send, other_y).start()

        @pl.when(from_left >= 0)
        def _():
            multiply(from_left, b)

        @pl.when(from_right < ctx)
        def _():
            multiply(from_right, b)

    def y_step(b):
        if ny == 1:
            return
        for step in range(nz):
            for toward in (-1, 1) if step > 0 else (1,):
                twin_z = z + toward * step

                @pl.when(jnp.logical_and(twin_z >= 0, twin_z < nz))
                def _():
                    slot = twin_z * ny + (1 - y)
                    along(slot, b, ay_send, other_y).wait_recv()
                    multiply(slot, b)

    def swap(b):
        return remote(
            acc.at[b, pl.ds(pl.multiple_of((1 - ci) * half, LANES), half), :],
            recv_c.at[b],
            csend.at[b],
            crecv.at[b],
            {"chan": 1 - ci},
        )

    def out_copy(q, b, source_slot):
        return remote(
            obuf.at[b, pl.ds(q * local_len, local_len), :],
            land.at[source_slot, b],
            osend.at[q, b],
            orecv.at[source_slot, b],
            {"ctx": ci * per + q, "chan": dest_chan},
        )

    def is_self(q):
        return jnp.logical_and(ci * per + q == me, dest_chan == ci)

    my_slot = lax.rem(me, per)

    def send_out(b):
        swap(b).wait()
        obuf[b] = (acc[b, mine, :] + recv_c[b]).astype(BF16)
        for q in range(per):

            @pl.when(jnp.logical_not(is_self(q)))
            def _():
                out_copy(q, b, my_slot).start()

            @pl.when(is_self(q))
            def _():
                land[my_slot, b] = obuf[b, q * local_len : (q + 1) * local_len, :]

    for b in range(genomes):
        for step in range(1, nz):
            if b == 0 or step == nz - 1:
                z_step(b, step)
            if step >= 2 and b + 1 < genomes:
                z_step(b + 1, step - 1)
        if b > 0:
            send_out(b - 1)
        y_step(b)
        swap(b).start()
    send_out(genomes - 1)

    for b in range(genomes):
        for q in range(per):

            @pl.when(jnp.logical_not(is_self(q)))
            def _():
                out_copy(q, b, q).wait_recv()

            out_ref[b, :, q * cols : (q + 1) * cols] = land[q, b]

    for off in range(1, ctx):
        remote(
            tok_ref, tok_all.at[me], tok_send.at[off], tok_recv.at[me], {"ctx": lax.rem(me + off, ctx)}
        ).wait_send()
    for h in range(pieces):
        for off in range(1, groups):
            group_copy(off, h, gi, lax.rem(gi + off, groups)).wait_send()
        for dz in range(nz):
            if ny == 2:
                y_copy(dz, h).wait_send()

            @pl.when(z < dz)
            def _():
                right_copy(dz, h).wait_send()

            @pl.when(z > dz)
            def _():
                left_copy(dz, h).wait_send()

    for b in range(genomes):
        for q in range(per):

            @pl.when(jnp.logical_not(is_self(q)))
            def _():
                out_copy(q, b, my_slot).wait_send()

        for dz in range(nz):
            slot = dz * ny + y

            @pl.when(jnp.logical_and(dz <= z, z < nz - 1))
            def _():
                along(slot, b, ar_send, right).wait_send()

            @pl.when(jnp.logical_and(dz >= z, z > 0))
            def _():
                along(slot, b, al_send, left).wait_send()

            if ny == 2:
                along(slot, b, ay_send, other_y).wait_send()


def body(
    groups,
    ctx,
    chans,
    tokens,
    embed_table,
    norm_gain,
    input_proj,
    short_filter,
    pole_rate,
    residue,
    skip_gain,
    output_proj,
):
    genomes, local_len = tokens.shape
    length = local_len * ctx
    features, branches, channels = input_proj.shape
    vocab = embed_table.shape[0]
    filter_count, poles = pole_rate.shape
    group_size = channels // filter_count
    share = channels // ctx
    filters = filter_count // ctx
    cols = output_proj.shape[1]
    rows = vocab // groups
    ny = 2 if ctx % 2 == 0 and ctx <= 8 else 1
    nz = ctx // ny
    taps = short_filter.shape[2]
    half = length // chans
    per = ctx // chans

    def padded(array):
        if share == LANES:
            return array
        cut = array.reshape(array.shape[:-1] + (ctx, share))
        pads = [(0, 0)] * (cut.ndim - 1) + [(0, LANES - share)]
        return jnp.pad(cut, pads).reshape(array.shape[:-1] + (ctx * LANES,))

    weights = padded(jnp.transpose(input_proj, (1, 0, 2)))
    out_weights = output_proj
    if share != LANES:
        out_weights = jnp.pad(
            output_proj.reshape(ctx, share, cols), ((0, 0), (0, LANES - share), (0, 0))
        ).reshape(ctx * LANES, cols)
    short = jnp.transpose(short_filter, (0, 2, 1))
    skip = padded(skip_gain).reshape(1, ctx * LANES)

    vmem = pl.BlockSpec(memory_space=pltpu.VMEM)
    dma = pltpu.SemaphoreType.DMA
    wide_lanes = 3 * LANES
    result = pl.pallas_call(
        functools.partial(kernel, (groups, ctx, chans, ny, group_size, filters)),
        out_shape=jax.ShapeDtypeStruct((genomes, local_len, cols * per), BF16),
        in_specs=[pl.BlockSpec(memory_space=pl.ANY)] * 9,
        out_specs=vmem,
        scratch_shapes=[
            pltpu.VMEM((genomes, local_len), jnp.int32),
            pltpu.VMEM((1, features), F32),
            pltpu.VMEM((branches, features, ctx * LANES), BF16),
            pltpu.VMEM((branches, taps, filter_count), F32),
            pltpu.VMEM((poles, filter_count), F32),
            pltpu.VMEM((poles, filter_count), F32),
            pltpu.VMEM((1, LANES), F32),
            pltpu.VMEM((ctx * LANES, cols), BF16),
            pltpu.VMEM((rows, features * ctx), BF16),
            pltpu.VMEM((rows, features), BF16),
            pltpu.VMEM((branches * taps, LANES), F32),
            pltpu.VMEM((ctx, genomes, local_len), jnp.int32),
            pltpu.VMEM((genomes, length, LANES), jnp.int32),
            pltpu.VMEM((nz, PIECES, rows // PIECES, wide_lanes), BF16),
            pltpu.VMEM((nz, PIECES, rows // PIECES, wide_lanes), F32),
            pltpu.VMEM((nz, PIECES, rows // PIECES, wide_lanes), BF16),
            pltpu.VMEM((nz, PIECES, rows // PIECES, wide_lanes), BF16),
            pltpu.VMEM((nz, PIECES, rows // PIECES, wide_lanes), BF16),
            pltpu.VMEM((nz, PIECES, rows // PIECES, wide_lanes), BF16),
            pltpu.VMEM((groups, PIECES, rows // PIECES, wide_lanes), BF16),
            pltpu.VMEM((filters, LANES, length), BF16),
            pltpu.VMEM((length, LANES), F32),
            pltpu.VMEM((ctx, genomes, length, LANES), BF16),
            pltpu.VMEM((genomes, length, cols), F32),
            pltpu.VMEM((genomes, half, cols), F32),
            pltpu.VMEM((genomes, half, cols), BF16),
            pltpu.VMEM((per, genomes, local_len, cols), BF16),
            pltpu.VMEM((vocab, cols), BF16),
            dma((ctx,)),
            dma((ctx,)),
            dma((nz, PIECES)),
            dma((nz, PIECES)),
            dma((nz, PIECES)),
            dma((nz, PIECES)),
            dma((nz, PIECES)),
            dma((groups, PIECES)),
            dma((groups, PIECES)),
            dma((ctx, genomes)),
            dma((ctx, genomes)),
            dma((ctx, genomes)),
            dma((ctx, genomes)),
            dma((genomes,)),
            dma((genomes,)),
            dma((per, genomes)),
            dma((per, genomes)),
            dma((10,)),
        ],
        compiler_params=pltpu.CompilerParams(
            collective_id=0, has_side_effects=True, vmem_limit_bytes=56 * 1024 * 1024
        ),
    )(
        tokens,
        norm_gain.reshape(1, features * ctx),
        weights,
        short,
        jnp.transpose(pole_rate),
        jnp.transpose(residue),
        skip,
        out_weights,
        embed_table,
    )
    return result


def solution(mesh):
    sizes = mesh.shape
    return jax.shard_map(
        functools.partial(body, sizes["groups"], sizes["ctx"], sizes["chan"]),
        mesh=mesh,
        in_specs=(
            P("groups", "ctx"),
            P(),
            P(),
            P("ctx", None, "chan"),
            P(None, "chan", None),
            P("chan", None),
            P("chan", None),
            P("chan"),
            P("chan", "ctx"),
        ),
        out_specs=P("groups", "ctx", "chan"),
        check_vma=False,
    )
```
